32 devices in a mesh: ka: 16 (over z, y, core), pa: 2 (over x).
Axes of the slice: x: 2, y: 2, z: 4, core: 2. Of those that a mesh axis runs over, the one named last changes fastest.
Arguments:
- conduction: bfloat16 [16, 48, 2048], P('ka'), may hold values from -6 to 6
- weighted: bfloat16 [16, 48, 2048], P('ka'), may hold values from -6 to 6
- valence: bfloat16 [16, 64, 2048], P('ka', None, 'pa'), may hold values from -0.03125 to 0.03125
- screening: bfloat16 [16, 2048, 2048], P('ka', None, 'pa'), may hold values from -0.125 to 0.125
- pair_transfer: int32 [16, 16], replicated, may hold values from 0 to 15, as said below
- owner_map: int32 [16], replicated, may hold values from 0 to 15, each once
Outputs:
- kernel_out: float32 [16, 48, 64], P('ka')
The draws below stay inside these ranges and needn't reach their ends.
Inputs may be any that keep to these rules, and one draw needn't show every extreme that they name: pair_transfer[i, j] = (g_i - g_j) mod 16 for positions g of the k-points on a cyclic grid of 16 points (a permutation drawn from the seed), so each row and each column names every transfer once. `owner_map`: each transfer is held by exactly one slot.
All inputs are finite; a program needn't handle non-finite values.
Results may differ from the reference program's by a relative error of at most 0.0029.
Values may be sent and summed in bfloat16 or wider, within the bound.
A program may use at most 128 MiB of HBM per device.

```python
import jax
import jax.numpy as jnp
from jax import lax

NB = 48
NV = 64
P_SIZE = 2048
NK = 16


def draw_pair_transfer(key, part):
    positions = jax.random.permutation(jax.random.fold_in(key, 11), NK)
    return jnp.mod(positions[:, None] - positions[None, :], NK).astype(jnp.int32)


def level_of(own_key, extent, split, least, high):
    def one(position, shards_of):
        steps = jax.random.uniform(jax.random.fold_in(jax.random.fold_in(own_key, 6), position), (shards_of,), jnp.float32, least / len(split), high / len(split))
        return jnp.repeat(jnp.exp(steps), extent[position] // shards_of).reshape((-1,) + (1,) * (len(extent) - position - 1))

    factor_of = one(*split[0])
    for cut in split[1:]:
        factor_of = factor_of * one(*cut)
    return factor_of


def noise(stream_key, dims, deviation, bound, pieces=(), held_as=jnp.bfloat16):
    array = deviation * jax.random.normal(stream_key, dims, jnp.float32)
    if pieces:
        array = array * level_of(stream_key, dims, pieces, -0.22, 0.18)
    return jnp.clip(array, -bound, bound).astype(held_as)


def setup_inputs(seed: int = 0) -> dict:
    streams_of = jax.random.split(jax.random.key(seed), 7)
    return {
        "conduction": noise(streams_of[0], (NK, NB, P_SIZE), 1.0, 6.0, ((0, 16),)),
        "weighted": noise(streams_of[1], (NK, NB, P_SIZE), 1.0, 6.0, ((0, 16),)),
        "valence": noise(streams_of[2], (NK, NV, P_SIZE), (P_SIZE * NK) ** -0.5, 0.03125, ((0, 16), (2, 2))),
        "screening": noise(streams_of[3], (NK, P_SIZE, P_SIZE), P_SIZE ** -0.5, 0.125, ((0, 16), (2, 2))),
        "pair_transfer": draw_pair_transfer(jax.random.fold_in(streams_of[6], 71), 0),
        "owner_map": jax.random.permutation(streams_of[5], NK).astype(jnp.int32),
    }


def reference(conduction, weighted, valence, screening, pair_transfer, owner_map):
    columns = jnp.arange(NK, dtype=jnp.int32)
    weighted_wide = weighted.astype(jnp.float32)

    def visit(total, slot):
        transfer = owner_map[slot]
        partners = jnp.sum(jnp.where(pair_transfer == transfer, columns[None, :], 0), axis=1).astype(jnp.int32)
        partner_cond = jnp.take(conduction, partners, axis=0).astype(jnp.float32)
        density = (partner_cond * weighted_wide).astype(jnp.bfloat16)
        screened = jnp.dot(density.reshape(NK * NB, P_SIZE), screening[slot], preferred_element_type=jnp.float32)
        return total + partner_cond * screened.reshape(NK, NB, P_SIZE), None

    folded, _ = lax.scan(visit, jnp.zeros((NK, NB, P_SIZE), jnp.float32), jnp.arange(NK, dtype=jnp.int32))
    return jnp.einsum("kbp,kvp->kbv", folded, valence.astype(jnp.float32), precision=lax.Precision.HIGHEST)
```

```python
import functools

import jax
import jax.numpy as jnp
from jax import lax
from jax.experimental import pallas as pl
from jax.experimental.pallas import tpu as pltpu
from jax.sharding import PartitionSpec as P

MESH = pl.DeviceIdType.MESH
TILE = 256


def kernel(
    nk, halves, pair_ref, owner_ref, cond_ref, wt_ref, val_ref, scr_ref, out_ref,
    cond_all, wt_all, val_all, scr, dens, acc, given, taken, partner,
    own_sem, scr_sem, z_send, z_recv, y_send, y_recv, x_send, x_recv, c_send, c_recv,
    end_send, end_recv,
):
    nb, half = cond_all.shape[2], cond_all.shape[3]
    nv = val_all.shape[1]
    n = nk // 4
    ka = lax.axis_index("ka")
    pa = lax.axis_index("pa")
    core = lax.rem(ka, 2)
    mid = lax.rem(ka // 2, 2)
    outer = ka // 4
    devices = nk * halves
    me = ka * halves + pa

    def point(o, m, c):
        return (o * 2 + m) * 2 + c

    upper = (2 * outer) // n
    shorter = outer * (1 - upper) + (n - 1 - outer) * upper

    def layer(t):
        near = (2 * lax.rem(t, 2) - 1) * ((t + 1) // 2)
        far = (1 - 2 * upper) * (t - shorter)
        beyond = (t - 1 - 2 * shorter + 2 * n) // (2 * n)
        return outer + near * (1 - beyond) + far * beyond

    own = []
    for h in range(halves):
        own.append(pltpu.make_async_copy(cond_ref.at[0, :, pl.ds(h * half, half)], cond_all.at[ka, h], own_sem.at[0, h]))
        own.append(pltpu.make_async_copy(wt_ref.at[0, :, pl.ds(h * half, half)], wt_all.at[ka, h], own_sem.at[1, h]))
    own.append(pltpu.make_async_copy(val_ref.at[0], val_all.at[ka], own_sem.at[2, 0]))
    for copy in own:
        copy.start()
    scr_copy = pltpu.make_async_copy(scr_ref.at[0], scr, scr_sem.at[0])
    scr_copy.start()

    barrier = pltpu.get_barrier_semaphore()

    @pl.loop(1, devices)
    def _(d):
        other = lax.rem(me + d, devices)
        pl.semaphore_signal(barrier, inc=1, device_id=(other // halves, lax.rem(other, halves)), device_id_type=MESH)

    pl.semaphore_wait(barrier, devices - 1)
    for copy in own:
        copy.wait()
    scr_copy.wait()

    def block(kind, o, m, c, h):
        if kind == 2:
            return val_all.at[point(o, m, c)]
        return (cond_all, wt_all)[kind].at[point(o, m, c), h]

    def remote(ref, send, recv, device):
        return pltpu.make_async_remote_copy(
            src_ref=ref, dst_ref=ref, send_sem=send, recv_sem=recv, device_id=device, device_id_type=MESH
        )

    def z_copy(kind, o, way):
        to = lax.rem(outer + (1 if way else n - 1), n)
        return remote(
            block(kind, o, mid, core, pa), z_send.at[kind, way, o], z_recv.at[kind, o], (point(to, mid, core), pa)
        )

    def y_copy(kind, o, m):
        return remote(
            block(kind, o, m, core, pa), y_send.at[kind, o], y_recv.at[kind, o], (point(outer, 1 - mid, core), pa)
        )

    def x_copy(kind, o, m, h):
        return remote(
            block(kind, o, m, core, h), x_send.at[kind, o, m], x_recv.at[kind, o, m], (ka, 1 - pa)
        )

    def c_copy(kind, o, m, c, h):
        slot = 0 if kind == 2 else h
        return remote(
            block(kind, o, m, c, h), c_send.at[kind, o, m, slot], c_recv.at[kind, o, m, slot],
            (point(outer, mid, 1 - core), pa),
        )

    def stage_a(kind, t):
        o = layer(t)

        @pl.when(t > 0)
        def _():
            z_copy(kind, o, 0).wait_recv()

        @pl.when((o <= outer) & (outer < n - 1))
        def _():
            z_copy(kind, o, 1).start()

        @pl.when((o >= outer) & (outer > 0))
        def _():
            z_copy(kind, o, 0).start()

        y_copy(kind, o, mid).start()
        if kind < 2:
            @pl.when(t > 0)
            def _():
                x_copy(kind, o, mid, pa).start()
        c_copy(kind, o, mid, core, pa).start()

    def stage_b(kind, t):
        o = layer(t)
        y_copy(kind, o, 1 - mid).wait_recv()
        if kind < 2:
            x_copy(kind, o, 1 - mid, pa).start()
        c_copy(kind, o, 1 - mid, core, pa).start()

    def stage_c(kind, t):
        if kind < 2:
            o = layer(t)
            for m in (mid, 1 - mid):
                @pl.when((t > 0) | (m != mid))
                def _():
                    x_copy(kind, o, m, 1 - pa).wait_recv()

                c_copy(kind, o, m, core, 1 - pa).start()

    def stage_d(kind, t):
        o = layer(t)
        for m in range(2):
            for h in range(1 if kind == 2 else halves):
                c_copy(kind, o, m, 1 - core, h).wait_recv()

    def end_copy(k, h):
        return pltpu.make_async_remote_copy(
            src_ref=given.at[k], dst_ref=taken.at[me], send_sem=end_send.at[k, h], recv_sem=end_recv.at[me],
            device_id=(k, h), device_id_type=MESH,
        )

    def compute(o):
        for q in range(4):
            k = o * 4 + q
            for h in range(halves):
                dens[q * nb:(q + 1) * nb, h * half:(h + 1) * half] = cond_all[partner[k], h] * wt_all[k, h]
        total = None
        for lo in range(0, half, TILE):
            cols = slice(lo, lo + TILE)
            screened = jnp.dot(dens[...], scr[:, cols], preferred_element_type=jnp.float32)
            terms = jnp.concatenate(
                [
                    (cond_all[partner[o * 4 + q], pa, :, cols].astype(jnp.float32) * screened[q * nb:(q + 1) * nb])
                    .astype(jnp.bfloat16)
                    for q in range(4)
                ],
                axis=0,
            )
            val = jnp.concatenate([val_all[o * 4 + q, :, cols] for q in range(4)], axis=0)
            part = lax.dot_general(terms, val, (((1,), (1,)), ((), ())), preferred_element_type=jnp.float32)
            total = part if total is None else total + part
        acc[...] = total

        first = lax.broadcasted_iota(jnp.int32, (nb // 2, 2 * nv), 1) < nv
        for q in range(4):
            k = o * 4 + q
            lanes = slice((q // 2) * 2 * nv, (q // 2 + 1) * 2 * nv)
            top = acc[q * nb:q * nb + nb // 2, lanes]
            low = acc[q * nb + nb // 2:(q + 1) * nb, lanes]
            if q % 2 == 0:
                packed = jnp.where(first, top, pltpu.roll(low, nv, 1))
            else:
                packed = jnp.where(first, pltpu.roll(top, nv, 1), low)
            given[k] = packed

    def staged(stage, u):
        @pl.when((u >= 0) & (u < n))
        def _():
            stage(0, u)

        @pl.when((u >= n) & (u < 2 * n))
        def _():
            stage(1, u - n)
            stage(2, u - n)

    @pl.loop(0, 2 * n + 3)
    def _(u):
        staged(stage_a, u)
        staged(stage_b, u - 1)
        staged(stage_c, u - 2)
        staged(stage_d, u - 3)

        @pl.when(u == 0)
        def _():
            held = owner_ref[ka]

            @pl.loop(0, nk)
            def _(i):
                partner[i] = lax.fori_loop(
                    0, nk, lambda j, found: jnp.where(pair_ref[i, j] == held, j, found), jnp.int32(0)
                )

    @pl.loop(0, n)
    def _(o):
        compute(o)

    @pl.loop(1, devices)
    def _(d):
        other = lax.rem(me + d, devices)
        end_copy(other // halves, lax.rem(other, halves)).start()

    @pl.loop(0, n)
    def _(o):
        for kind in range(3):
            @pl.when((o <= outer) & (outer < n - 1))
            def _():
                z_copy(kind, o, 1).wait_send()

            @pl.when((o >= outer) & (outer > 0))
            def _():
                z_copy(kind, o, 0).wait_send()

            y_copy(kind, o, mid).wait_send()
            for m in range(2):
                if kind < 2:
                    @pl.when((o != outer) | (m != mid))
                    def _():
                        x_copy(kind, o, m, pa).wait_send()

                for h in range(1 if kind == 2 else halves):
                    c_copy(kind, o, m, core, h).wait_send()

    @pl.loop(0, devices)
    def _(d):
        k, h = d // halves, lax.rem(d, halves)

        @pl.when(d != me)
        def _():
            end_copy(k, h).wait_send()
            pltpu.make_async_remote_copy(
                src_ref=given.at[k], dst_ref=taken.at[d], send_sem=end_send.at[k, h], recv_sem=end_recv.at[d],
                device_id=(k, h), device_id_type=MESH,
            ).wait_recv()

    total = lax.fori_loop(1, devices, lambda d, s: s + taken[lax.rem(me + d, devices)], given[ka])
    out_ref[0, :nb // 2, :] = total[:, :nv]
    out_ref[0, nb // 2:, :] = pltpu.roll(total, nv, 1)[:, :nv]


def shards(nk, halves, conduction, weighted, valence, screening, pair_transfer, owner_map):
    nb, width = conduction.shape[1:]
    nv, half = valence.shape[1:]
    n = nk // 4
    devices = nk * halves
    bf16, f32 = jnp.bfloat16, jnp.float32
    dma = pltpu.SemaphoreType.DMA
    smem = pl.BlockSpec(memory_space=pltpu.SMEM)
    anywhere = pl.BlockSpec(memory_space=pl.ANY)
    return pl.pallas_call(
        functools.partial(kernel, nk, halves),
        out_shape=jax.ShapeDtypeStruct((1, nb, nv), f32),
        in_specs=[smem, smem, anywhere, anywhere, anywhere, anywhere],
        out_specs=pl.BlockSpec(memory_space=pltpu.VMEM),
        scratch_shapes=[
            pltpu.VMEM((nk, halves, nb, half), bf16),
            pltpu.VMEM((nk, halves, nb, half), bf16),
            pltpu.VMEM((nk, nv, half), bf16),
            pltpu.VMEM((width, half), bf16),
            pltpu.VMEM((4 * nb, width), bf16),
            pltpu.VMEM((4 * nb, 4 * nv), f32),
            pltpu.VMEM((nk, nb // 2, 2 * nv), f32),
            pltpu.VMEM((devices, nb // 2, 2 * nv), f32),
            pltpu.SMEM((nk,), jnp.int32),
            dma((3, halves)),
            dma((1,)),
            dma((3, 2, n)),
            dma((3, n)),
            dma((3, n)),
            dma((3, n)),
            dma((2, n, 2)),
            dma((2, n, 2)),
            dma((3, n, 2, halves)),
            dma((3, n, 2, halves)),
            dma((nk, halves)),
            dma((devices,)),
        ],
        compiler_params=pltpu.CompilerParams(
            collective_id=0, has_side_effects=True, vmem_limit_bytes=56 * 1024 * 1024
        ),
    )(pair_transfer, owner_map, conduction, weighted, valence, screening)


def solution(mesh):
    in_specs = (
        P("ka", None, None),
        P("ka", None, None),
        P("ka", None, "pa"),
        P("ka", None, "pa"),
        P(),
        P(),
    )
    body = functools.partial(shards, mesh.shape["ka"], mesh.shape["pa"])
    return jax.shard_map(body, mesh=mesh, in_specs=in_specs, out_specs=P("ka", None, None), check_vma=False)
```

```python
import functools

import jax
import jax.numpy as jnp
from jax import lax
from jax.experimental import pallas as pl
from jax.experimental.pallas import tpu as pltpu
from jax.sharding import PartitionSpec as P

MESH = pl.DeviceIdType.MESH
TILE = 256


def kernel(
    nk, halves, pair_ref, owner_ref, cond_ref, wt_ref, val_ref, scr_ref, out_ref,
    cond_all, wt_all, val_all, scr, dens, terms, acc, given, taken, partner,
    own_sem, scr_sem, z_send, z_recv, y_send, y_recv, x_send, x_recv, c_send, c_recv,
    end_send, end_recv,
):
    nb, half = cond_all.shape[2], cond_all.shape[3]
    nv = val_all.shape[1]
    n = nk // 4
    ka = lax.axis_index("ka")
    pa = lax.axis_index("pa")
    core = lax.rem(ka, 2)
    mid = lax.rem(ka // 2, 2)
    outer = ka // 4
    devices = nk * halves
    me = ka * halves + pa

    def point(o, m, c):
        return (o * 2 + m) * 2 + c

    upper = (2 * outer) // n
    shorter = outer * (1 - upper) + (n - 1 - outer) * upper

    def layer(t):
        near = (2 * lax.rem(t, 2) - 1) * ((t + 1) // 2)
        far = (1 - 2 * upper) * (t - shorter)
        beyond = (t - 1 - 2 * shorter + 2 * n) // (2 * n)
        return outer + near * (1 - beyond) + far * beyond

    own = []
    for h in range(halves):
        own.append(pltpu.make_async_copy(cond_ref.at[0, :, pl.ds(h * half, half)], cond_all.at[ka, h], own_sem.at[0, h]))
        own.append(pltpu.make_async_copy(wt_ref.at[0, :, pl.ds(h * half, half)], wt_all.at[ka, h], own_sem.at[1, h]))
    own.append(pltpu.make_async_copy(val_ref.at[0], val_all.at[ka], own_sem.at[2, 0]))
    for copy in own:
        copy.start()
    scr_copy = pltpu.make_async_copy(scr_ref.at[0], scr, scr_sem.at[0])
    scr_copy.start()

    barrier = pltpu.get_barrier_semaphore()

    @pl.loop(1, devices)
    def _(d):
        other = lax.rem(me + d, devices)
        pl.semaphore_signal(barrier, inc=1, device_id=(other // halves, lax.rem(other, halves)), device_id_type=MESH)

    pl.semaphore_wait(barrier, devices - 1)
    for copy in own:
        copy.wait()
    scr_copy.wait()

    def block(kind, o, m, c, h):
        if kind == 2:
            return val_all.at[point(o, m, c)]
        return (cond_all, wt_all)[kind].at[point(o, m, c), h]

    def remote(ref, send, recv, device):
        return pltpu.make_async_remote_copy(
            src_ref=ref, dst_ref=ref, send_sem=send, recv_sem=recv, device_id=device, device_id_type=MESH
        )

    def z_copy(kind, o, way):
        to = lax.rem(outer + (1 if way else n - 1), n)
        return remote(
            block(kind, o, mid, core, pa), z_send.at[kind, way, o], z_recv.at[kind, o], (point(to, mid, core), pa)
        )

    def y_copy(kind, o, m):
        return remote(
            block(kind, o, m, core, pa), y_send.at[kind, o], y_recv.at[kind, o], (point(outer, 1 - mid, core), pa)
        )

    def x_copy(kind, o, m, h):
        return remote(
            block(kind, o, m, core, h), x_send.at[kind, o, m], x_recv.at[kind, o, m], (ka, 1 - pa)
        )

    def c_copy(kind, o, m, c, h):
        slot = 0 if kind == 2 else h
        return remote(
            block(kind, o, m, c, h), c_send.at[kind, o, m, slot], c_recv.at[kind, o, m, slot],
            (point(outer, mid, 1 - core), pa),
        )

    def stage_a(kind, t):
        o = layer(t)

        @pl.when(t > 0)
        def _():
            z_copy(kind, o, 0).wait_recv()

        @pl.when((o <= outer) & (outer < n - 1))
        def _():
            z_copy(kind, o, 1).start()

        @pl.when((o >= outer) & (outer > 0))
        def _():
            z_copy(kind, o, 0).start()

        y_copy(kind, o, mid).start()
        if kind < 2:
            @pl.when(t > 0)
            def _():
                x_copy(kind, o, mid, pa).start()
        c_copy(kind, o, mid, core, pa).start()

    def stage_b(kind, t):
        o = layer(t)
        y_copy(kind, o, 1 - mid).wait_recv()
        if kind < 2:
            x_copy(kind, o, 1 - mid, pa).start()
        c_copy(kind, o, 1 - mid, core, pa).start()

    def stage_c(kind, t):
        if kind < 2:
            o = layer(t)
            for m in (mid, 1 - mid):
                @pl.when((t > 0) | (m != mid))
                def _():
                    x_copy(kind, o, m, 1 - pa).wait_recv()

                c_copy(kind, o, m, core, 1 - pa).start()

    def stage_d(kind, t):
        o = layer(t)
        for m in range(2):
            for h in range(1 if kind == 2 else halves):
                c_copy(kind, o, m, 1 - core, h).wait_recv()

    def end_copy(k, h):
        return pltpu.make_async_remote_copy(
            src_ref=given.at[k], dst_ref=taken.at[me], send_sem=end_send.at[k, h], recv_sem=end_recv.at[me],
            device_id=(k, h), device_id_type=MESH,
        )

    def fold(o):
        for q in range(4):
            k = o * 4 + q
            for h in range(halves):
                dens[q * nb:(q + 1) * nb, h * half:(h + 1) * half] = cond_all[partner[k], h] * wt_all[k, h]
        for lo in range(0, half, TILE):
            cols = slice(lo, lo + TILE)
            screened = jnp.dot(dens[...], scr[:, cols], preferred_element_type=jnp.float32)
            for q in range(4):
                k = o * 4 + q
                terms[o, q * nb:(q + 1) * nb, cols] = (
                    cond_all[partner[k], pa, :, cols].astype(jnp.float32) * screened[q * nb:(q + 1) * nb]
                ).astype(jnp.bfloat16)

    def contract(o):
        val = jnp.concatenate([val_all[o * 4 + q] for q in range(4)], axis=0)
        acc[...] = lax.dot_general(terms[o], val, (((1,), (1,)), ((), ())), preferred_element_type=jnp.float32)
        first = lax.broadcasted_iota(jnp.int32, (nb // 2, 2 * nv), 1) < nv
        for q in range(4):
            k = o * 4 + q
            lanes = slice((q // 2) * 2 * nv, (q // 2 + 1) * 2 * nv)
            top = acc[q * nb:q * nb + nb // 2, lanes]
            low = acc[q * nb + nb // 2:(q + 1) * nb, lanes]
            if q % 2 == 0:
                packed = jnp.where(first, top, pltpu.roll(low, nv, 1))
            else:
                packed = jnp.where(first, pltpu.roll(top, nv, 1), low)
            given[k] = packed

    def staged(stage, u):
        @pl.when((u >= 0) & (u < n))
        def _():
            stage(0, u)

        @pl.when((u >= n) & (u < 2 * n))
        def _():
            stage(1, u - n)

        @pl.when((u >= 2 * n) & (u < 3 * n))
        def _():
            stage(2, u - 2 * n)

    @pl.loop(0, 3 * n + 3)
    def _(u):
        staged(stage_a, u)
        staged(stage_b, u - 1)
        staged(stage_c, u - 2)
        staged(stage_d, u - 3)

        @pl.when(u == 0)
        def _():
            held = owner_ref[ka]

            @pl.loop(0, nk)
            def _(i):
                partner[i] = lax.fori_loop(
                    0, nk, lambda j, found: jnp.where(pair_ref[i, j] == held, j, found), jnp.int32(0)
                )

        @pl.when(u >= 2 * n + 3)
        def _():
            fold(u - 2 * n - 3)

    @pl.loop(0, n)
    def _(o):
        contract(o)

    @pl.loop(1, devices)
    def _(d):
        other = lax.rem(me + d, devices)
        end_copy(other // halves, lax.rem(other, halves)).start()

    @pl.loop(0, n)
    def _(o):
        for kind in range(3):
            @pl.when((o <= outer) & (outer < n - 1))
            def _():
                z_copy(kind, o, 1).wait_send()

            @pl.when((o >= outer) & (outer > 0))
            def _():
                z_copy(kind, o, 0).wait_send()

            y_copy(kind, o, mid).wait_send()
            for m in range(2):
                if kind < 2:
                    @pl.when((o != outer) | (m != mid))
                    def _():
                        x_copy(kind, o, m, pa).wait_send()

                for h in range(1 if kind == 2 else halves):
                    c_copy(kind, o, m, core, h).wait_send()

    @pl.loop(0, devices)
    def _(d):
        k, h = d // halves, lax.rem(d, halves)

        @pl.when(d != me)
        def _():
            end_copy(k, h).wait_send()
            pltpu.make_async_remote_copy(
                src_ref=given.at[k], dst_ref=taken.at[d], send_sem=end_send.at[k, h], recv_sem=end_recv.at[d],
                device_id=(k, h), device_id_type=MESH,
            ).wait_recv()

    total = lax.fori_loop(1, devices, lambda d, s: s + taken[lax.rem(me + d, devices)], given[ka])
    out_ref[0, :nb // 2, :] = total[:, :nv]
    out_ref[0, nb // 2:, :] = pltpu.roll(total, nv, 1)[:, :nv]


def shards(nk, halves, conduction, weighted, valence, screening, pair_transfer, owner_map):
    nb, width = conduction.shape[1:]
    nv, half = valence.shape[1:]
    n = nk // 4
    devices = nk * halves
    bf16, f32 = jnp.bfloat16, jnp.float32
    dma = pltpu.SemaphoreType.DMA
    smem = pl.BlockSpec(memory_space=pltpu.SMEM)
    anywhere = pl.BlockSpec(memory_space=pl.ANY)
    return pl.pallas_call(
        functools.partial(kernel, nk, halves),
        out_shape=jax.ShapeDtypeStruct((1, nb, nv), f32),
        in_specs=[smem, smem, anywhere, anywhere, anywhere, anywhere],
        out_specs=pl.BlockSpec(memory_space=pltpu.VMEM),
        scratch_shapes=[
            pltpu.VMEM((nk, halves, nb, half), bf16),
            pltpu.VMEM((nk, halves, nb, half), bf16),
            pltpu.VMEM((nk, nv, half), bf16),
            pltpu.VMEM((width, half), bf16),
            pltpu.VMEM((4 * nb, width), bf16),
            pltpu.VMEM((n, 4 * nb, half), bf16),
            pltpu.VMEM((4 * nb, 4 * nv), f32),
            pltpu.VMEM((nk, nb // 2, 2 * nv), f32),
            pltpu.VMEM((devices, nb // 2, 2 * nv), f32),
            pltpu.SMEM((nk,), jnp.int32),
            dma((3, halves)),
            dma((1,)),
            dma((3, 2, n)),
            dma((3, n)),
            dma((3, n)),
            dma((3, n)),
            dma((2, n, 2)),
            dma((2, n, 2)),
            dma((3, n, 2, halves)),
            dma((3, n, 2, halves)),
            dma((nk, halves)),
            dma((devices,)),
        ],
        compiler_params=pltpu.CompilerParams(
            collective_id=0, has_side_effects=True, vmem_limit_bytes=56 * 1024 * 1024
        ),
    )(pair_transfer, owner_map, conduction, weighted, valence, screening)


def solution(mesh):
    in_specs = (
        P("ka", None, None),
        P("ka", None, None),
        P("ka", None, "pa"),
        P("ka", None, "pa"),
        P(),
        P(),
    )
    body = functools.partial(shards, mesh.shape["ka"], mesh.shape["pa"])
    return jax.shard_map(body, mesh=mesh, in_specs=in_specs, out_specs=P("ka", None, None), check_vma=False)
```

```python
import functools

import jax
import jax.numpy as jnp
from jax import lax
from jax.experimental import pallas as pl
from jax.experimental.pallas import tpu as pltpu
from jax.sharding import PartitionSpec as P

MESH = pl.DeviceIdType.MESH
TILE = 256


def kernel(
    nk, halves, pair_ref, owner_ref, cond_ref, wt_ref, val_ref, scr_ref, out_ref,
    cond_all, wt_all, val_all, scr, dens, terms, acc, given, taken, partner,
    own_sem, scr_sem, z_send, z_recv, y_send, y_recv, x_send, x_recv, c_send, c_recv,
    end_send, end_recv,
):
    nb, half = cond_all.shape[2], cond_all.shape[3]
    nv = val_all.shape[1]
    n = nk // 4
    ka = lax.axis_index("ka")
    pa = lax.axis_index("pa")
    core = lax.rem(ka, 2)
    mid = lax.rem(ka // 2, 2)
    outer = ka // 4
    devices = nk * halves
    me = ka * halves + pa

    def point(o, m, c):
        return (o * 2 + m) * 2 + c

    upper = (2 * outer) // n
    shorter = outer * (1 - upper) + (n - 1 - outer) * upper

    def layer(t):
        near = (2 * lax.rem(t, 2) - 1) * ((t + 1) // 2)
        far = (1 - 2 * upper) * (t - shorter)
        beyond = (t - 1 - 2 * shorter + 2 * n) // (2 * n)
        return outer + near * (1 - beyond) + far * beyond

    own = []
    for h in range(halves):
        own.append(pltpu.make_async_copy(cond_ref.at[0, :, pl.ds(h * half, half)], cond_all.at[ka, h], own_sem.at[0, h]))
        own.append(pltpu.make_async_copy(wt_ref.at[0, :, pl.ds(h * half, half)], wt_all.at[ka, h], own_sem.at[1, h]))
    own.append(pltpu.make_async_copy(val_ref.at[0], val_all.at[ka], own_sem.at[2, 0]))
    for copy in own:
        copy.start()
    scr_copy = pltpu.make_async_copy(scr_ref.at[0], scr, scr_sem.at[0])
    scr_copy.start()

    barrier = pltpu.get_barrier_semaphore()

    @pl.loop(1, devices)
    def _(d):
        other = lax.rem(me + d, devices)
        pl.semaphore_signal(barrier, inc=1, device_id=(other // halves, lax.rem(other, halves)), device_id_type=MESH)

    pl.semaphore_wait(barrier, devices - 1)
    for copy in own:
        copy.wait()
    scr_copy.wait()

    def block(kind, o, m, c, h):
        if kind == 2:
            return val_all.at[point(o, m, c)]
        return (cond_all, wt_all)[kind].at[point(o, m, c), h]

    def remote(ref, send, recv, device):
        return pltpu.make_async_remote_copy(
            src_ref=ref, dst_ref=ref, send_sem=send, recv_sem=recv, device_id=device, device_id_type=MESH
        )

    def z_copy(kind, o, way):
        to = lax.rem(outer + (1 if way else n - 1), n)
        return remote(
            block(kind, o, mid, core, pa), z_send.at[kind, way, o], z_recv.at[kind, o], (point(to, mid, core), pa)
        )

    def y_copy(kind, o, m):
        return remote(
            block(kind, o, m, core, pa), y_send.at[kind, o], y_recv.at[kind, o], (point(outer, 1 - mid, core), pa)
        )

    def x_copy(kind, o, m, h):
        return remote(
            block(kind, o, m, core, h), x_send.at[kind, o, m], x_recv.at[kind, o, m], (ka, 1 - pa)
        )

    def c_copy(kind, o, m, c, h):
        slot = 0 if kind == 2 else h
        return remote(
            block(kind, o, m, c, h), c_send.at[kind, o, m, slot], c_recv.at[kind, o, m, slot],
            (point(outer, mid, 1 - core), pa),
        )

    def stage_a(kind, t):
        o = layer(t)

        @pl.when(t > 0)
        def _():
            z_copy(kind, o, 0).wait_recv()

        @pl.when((o <= outer) & (outer < n - 1))
        def _():
            z_copy(kind, o, 1).start()

        @pl.when((o >= outer) & (outer > 0))
        def _():
            z_copy(kind, o, 0).start()

        y_copy(kind, o, mid).start()
        if kind < 2:
            @pl.when(t > 0)
            def _():
                x_copy(kind, o, mid, pa).start()
        c_copy(kind, o, mid, core, pa).start()

    def stage_b(kind, t):
        o = layer(t)
        y_copy(kind, o, 1 - mid).wait_recv()
        if kind < 2:
            x_copy(kind, o, 1 - mid, pa).start()
        c_copy(kind, o, 1 - mid, core, pa).start()

    def stage_c(kind, t):
        if kind < 2:
            o = layer(t)
            for m in (mid, 1 - mid):
                @pl.when((t > 0) | (m != mid))
                def _():
                    x_copy(kind, o, m, 1 - pa).wait_recv()

                c_copy(kind, o, m, core, 1 - pa).start()

    def stage_d(kind, t):
        o = layer(t)
        for m in range(2):
            for h in range(1 if kind == 2 else halves):
                c_copy(kind, o, m, 1 - core, h).wait_recv()

    def end_copy(k, h):
        return pltpu.make_async_remote_copy(
            src_ref=given.at[k], dst_ref=taken.at[me], send_sem=end_send.at[k, h], recv_sem=end_recv.at[me],
            device_id=(k, h), device_id_type=MESH,
        )

    def fold(o):
        for q in range(4):
            k = o * 4 + q
            for h in range(halves):
                dens[q * nb:(q + 1) * nb, h * half:(h + 1) * half] = cond_all[partner[k], h] * wt_all[k, h]
        for lo in range(0, half, TILE):
            cols = slice(lo, lo + TILE)
            screened = jnp.dot(dens[...], scr[:, cols], preferred_element_type=jnp.float32)
            for q in range(4):
                k = o * 4 + q
                terms[o, q * nb:(q + 1) * nb, cols] = (
                    cond_all[partner[k], pa, :, cols].astype(jnp.float32) * screened[q * nb:(q + 1) * nb]
                ).astype(jnp.bfloat16)

    def contract(o):
        val = jnp.concatenate([val_all[o * 4 + q] for q in range(4)], axis=0)
        acc[...] = lax.dot_general(terms[o], val, (((1,), (1,)), ((), ())), preferred_element_type=jnp.float32)
        first = lax.broadcasted_iota(jnp.int32, (nb // 2, 2 * nv), 1) < nv
        for q in range(4):
            k = o * 4 + q
            lanes = slice((q // 2) * 2 * nv, (q // 2 + 1) * 2 * nv)
            top = acc[q * nb:q * nb + nb // 2, lanes]
            low = acc[q * nb + nb // 2:(q + 1) * nb, lanes]
            if q % 2 == 0:
                packed = jnp.where(first, top, pltpu.roll(low, nv, 1))
            else:
                packed = jnp.where(first, pltpu.roll(top, nv, 1), low)
            given[k] = packed

    def staged(stage, u):
        @pl.when((u >= 0) & (u < n))
        def _():
            stage(0, u)

        @pl.when((u >= n) & (u < 2 * n))
        def _():
            stage(1, u - n)

    def valence_staged(stage, u):
        @pl.when((u >= n) & (u < 2 * n))
        def _():
            stage(2, u - n)

    @pl.loop(0, 2 * n + 3)
    def _(u):
        staged(stage_a, u)
        staged(stage_b, u - 1)
        valence_staged(stage_a, u - 1)
        staged(stage_c, u - 2)
        valence_staged(stage_b, u - 2)
        staged(stage_d, u - 3)

        @pl.when(u == 0)
        def _():
            held = owner_ref[ka]

            @pl.loop(0, nk)
            def _(i):
                partner[i] = lax.fori_loop(
                    0, nk, lambda j, found: jnp.where(pair_ref[i, j] == held, j, found), jnp.int32(0)
                )

    @pl.loop(0, n)
    def _(o):
        fold(o)

    @pl.loop(0, n)
    def _(t):
        stage_d(2, t)

    @pl.loop(0, n)
    def _(o):
        contract(o)

    @pl.loop(1, devices)
    def _(d):
        other = lax.rem(me + d, devices)
        end_copy(other // halves, lax.rem(other, halves)).start()

    @pl.loop(0, n)
    def _(o):
        for kind in range(3):
            @pl.when((o <= outer) & (outer < n - 1))
            def _():
                z_copy(kind, o, 1).wait_send()

            @pl.when((o >= outer) & (outer > 0))
            def _():
                z_copy(kind, o, 0).wait_send()

            y_copy(kind, o, mid).wait_send()
            for m in range(2):
                if kind < 2:
                    @pl.when((o != outer) | (m != mid))
                    def _():
                        x_copy(kind, o, m, pa).wait_send()

                for h in range(1 if kind == 2 else halves):
                    c_copy(kind, o, m, core, h).wait_send()

    @pl.loop(0, devices)
    def _(d):
        k, h = d // halves, lax.rem(d, halves)

        @pl.when(d != me)
        def _():
            end_copy(k, h).wait_send()
            pltpu.make_async_remote_copy(
                src_ref=given.at[k], dst_ref=taken.at[d], send_sem=end_send.at[k, h], recv_sem=end_recv.at[d],
                device_id=(k, h), device_id_type=MESH,
            ).wait_recv()

    total = lax.fori_loop(1, devices, lambda d, s: s + taken[lax.rem(me + d, devices)], given[ka])
    out_ref[0, :nb // 2, :] = total[:, :nv]
    out_ref[0, nb // 2:, :] = pltpu.roll(total, nv, 1)[:, :nv]


def shards(nk, halves, conduction, weighted, valence, screening, pair_transfer, owner_map):
    nb, width = conduction.shape[1:]
    nv, half = valence.shape[1:]
    n = nk // 4
    devices = nk * halves
    bf16, f32 = jnp.bfloat16, jnp.float32
    dma = pltpu.SemaphoreType.DMA
    smem = pl.BlockSpec(memory_space=pltpu.SMEM)
    anywhere = pl.BlockSpec(memory_space=pl.ANY)
    return pl.pallas_call(
        functools.partial(kernel, nk, halves),
        out_shape=jax.ShapeDtypeStruct((1, nb, nv), f32),
        in_specs=[smem, smem, anywhere, anywhere, anywhere, anywhere],
        out_specs=pl.BlockSpec(memory_space=pltpu.VMEM),
        scratch_shapes=[
            pltpu.VMEM((nk, halves, nb, half), bf16),
            pltpu.VMEM((nk, halves, nb, half), bf16),
            pltpu.VMEM((nk, nv, half), bf16),
            pltpu.VMEM((width, half), bf16),
            pltpu.VMEM((4 * nb, width), bf16),
            pltpu.VMEM((n, 4 * nb, half), bf16),
            pltpu.VMEM((4 * nb, 4 * nv), f32),
            pltpu.VMEM((nk, nb // 2, 2 * nv), f32),
            pltpu.VMEM((devices, nb // 2, 2 * nv), f32),
            pltpu.SMEM((nk,), jnp.int32),
            dma((3, halves)),
            dma((1,)),
            dma((3, 2, n)),
            dma((3, n)),
            dma((3, n)),
            dma((3, n)),
            dma((2, n, 2)),
            dma((2, n, 2)),
            dma((3, n, 2, halves)),
            dma((3, n, 2, halves)),
            dma((nk, halves)),
            dma((devices,)),
        ],
        compiler_params=pltpu.CompilerParams(
            collective_id=0, has_side_effects=True, vmem_limit_bytes=56 * 1024 * 1024
        ),
    )(pair_transfer, owner_map, conduction, weighted, valence, screening)


def solution(mesh):
    in_specs = (
        P("ka", None, None),
        P("ka", None, None),
        P("ka", None, "pa"),
        P("ka", None, "pa"),
        P(),
        P(),
    )
    body = functools.partial(shards, mesh.shape["ka"], mesh.shape["pa"])
    return jax.shard_map(body, mesh=mesh, in_specs=in_specs, out_specs=P("ka", None, None), check_vma=False)
```
